32 devices in a mesh: seq: 8 (over y, x, core), tp: 4 (over z).
Axes of the slice: x: 2, y: 2, z: 4, core: 2. Of those that a mesh axis runs over, the one named last changes fastest.
Arguments:
- tokens: bfloat16 [3072, 4096], P('seq'), may hold values from -14 to 14
- w_query: bfloat16 [4096, 4096], P(None, 'tp'), may hold values from -0.09375 to 0.09375
- w_key: bfloat16 [4096, 4096], P(None, 'tp'), may hold values from -0.09375 to 0.09375
- w_value: bfloat16 [4096, 4096], P(None, 'tp'), may hold values from -0.09375 to 0.09375
- grad_out: bfloat16 [3072, 4096], P('seq', 'tp'), may hold values from -6 to 6
Outputs:
- grad_tokens: bfloat16 [3072, 4096], P('seq')
The draws below stay inside these ranges and needn't reach their ends.
All inputs are finite; a program needn't handle non-finite values.
Results may differ from the reference program's by a relative error of at most 0.03.
Values may be sent and summed in bfloat16 or wider, within the bound.
No kernel may reach another device: no remote copies, remote signals or barrier semaphores. Data moves between devices by JAX's collectives and lax.ppermute only.
A program may use at most 128 MiB of HBM per device.

```python
import jax
import jax.numpy as jnp
from jax import lax

D = 4096
HEADS = 32
HEAD = 128
TOK_DEV = 384
TOKENS = 3072
N_SEQ = 8


def draw_tokens(key, part):
    key = jax.random.fold_in(key, 7)
    base_key = jax.random.fold_in(key, 0)
    values = jax.random.truncated_normal(base_key, -6.0, 6.0, (TOKENS, D), jnp.float32)
    return values.astype(jnp.bfloat16)


def shard_levels(own_key, shape, cuts, smallest, top_value):
    def one(axis_at, parts):
        draws = jax.random.uniform(jax.random.fold_in(jax.random.fold_in(own_key, 6), axis_at), (parts,), jnp.float32, smallest / len(cuts), top_value / len(cuts))
        return jnp.repeat(jnp.exp(draws), shape[axis_at] // parts).reshape((-1,) + (1,) * (len(shape) - axis_at - 1))

    factor_of = one(*cuts[0])
    for cut in cuts[1:]:
        factor_of = factor_of * one(*cut)
    return factor_of


def scatter_about(rng, shape, spread, reach, cuts=(), kind=jnp.bfloat16):
    entries = spread * jax.random.normal(rng, shape, jnp.float32)
    if cuts:
        entries = entries * shard_levels(rng, shape, cuts, -0.22, 0.18)
    return jnp.clip(entries, -reach, reach).astype(kind)


def setup_inputs(seed: int = 0) -> dict:
    streams_of = jax.random.split(jax.random.key(seed), 6)
    return {
        "tokens": draw_tokens(jax.random.fold_in(streams_of[5], 71), 0),
        "w_query": scatter_about(streams_of[1], (D, HEADS * HEAD), D ** -0.5, 0.09375, ((1, 4),)),
        "w_key": scatter_about(streams_of[2], (D, HEADS * HEAD), D ** -0.5, 0.09375, ((1, 4),)),
        "w_value": scatter_about(streams_of[3], (D, HEADS * HEAD), D ** -0.5, 0.09375, ((1, 4),)),
        "grad_out": scatter_about(streams_of[4], (TOKENS, HEADS * HEAD), 1.0, 6.0, ((0, 8), (1, 4))),
    }


def reference(tokens, w_query, w_key, w_value, grad_out):
    score_scale = HEAD ** -0.5
    queries = jnp.dot(tokens, w_query, preferred_element_type=jnp.float32).astype(jnp.bfloat16)
    keys_all = jnp.dot(tokens, w_key, preferred_element_type=jnp.float32).astype(jnp.bfloat16)
    values_all = jnp.dot(tokens, w_value, preferred_element_type=jnp.float32).astype(jnp.bfloat16)
    positions = jnp.arange(TOKENS, dtype=jnp.int32)
    times = (positions % TOK_DEV) * N_SEQ + positions // TOK_DEV
    allowed = times[None, :] <= times[:, None]

    def one_head(head):
        start = (head * HEAD).astype(jnp.int32)
        query_h = lax.dynamic_slice_in_dim(queries, start, HEAD, 1)
        key_h = lax.dynamic_slice_in_dim(keys_all, start, HEAD, 1)
        value_h = lax.dynamic_slice_in_dim(values_all, start, HEAD, 1)
        grad_h = lax.dynamic_slice_in_dim(grad_out, start, HEAD, 1)
        scores = jnp.dot(query_h, key_h.T, preferred_element_type=jnp.float32) * score_scale
        scores = jnp.where(allowed, scores, -1e30)
        top = jnp.max(scores, axis=1, keepdims=True)
        weights = jnp.exp(scores - top)
        total = jnp.sum(weights, axis=1, keepdims=True)
        logsum = top + jnp.log(total)
        attended = (jnp.dot(weights.astype(jnp.bfloat16), value_h, preferred_element_type=jnp.float32) / total).astype(jnp.bfloat16)
        row_delta = jnp.sum(grad_h.astype(jnp.float32) * attended.astype(jnp.float32), axis=1, keepdims=True)
        probs = jnp.exp(scores - logsum)
        grad_value = jnp.dot(probs.astype(jnp.bfloat16).T, grad_h, preferred_element_type=jnp.float32)
        grad_probs = jnp.dot(grad_h, value_h.T, preferred_element_type=jnp.float32)
        grad_scores = (probs * (grad_probs - row_delta)).astype(jnp.bfloat16)
        grad_query = jnp.dot(grad_scores, key_h, preferred_element_type=jnp.float32) * score_scale
        grad_key = jnp.dot(grad_scores.T, query_h, preferred_element_type=jnp.float32) * score_scale
        return grad_query, grad_key, grad_value

    grad_query, grad_key, grad_value = lax.map(one_head, jnp.arange(HEADS, dtype=jnp.int32))

    def merge_heads(stacked):
        return jnp.transpose(stacked, (1, 0, 2)).reshape(TOKENS, HEADS * HEAD).astype(jnp.bfloat16)

    partial_sum = jnp.dot(merge_heads(grad_query), w_query.T, preferred_element_type=jnp.float32)
    partial_sum = partial_sum + jnp.dot(merge_heads(grad_key), w_key.T, preferred_element_type=jnp.float32)
    partial_sum = partial_sum + jnp.dot(merge_heads(grad_value), w_value.T, preferred_element_type=jnp.float32)
    return partial_sum.astype(jnp.bfloat16)
```

```python
import functools
import math

import jax
import jax.numpy as jnp
from jax import lax
from jax.experimental import pallas as pl
from jax.experimental.pallas import tpu as pltpu
from jax.sharding import PartitionSpec as P

HEAD = 128
SPAN = 64
CHUNKS = 3
PIECE = 1024
UNIT = 256
LOW = -1e30
MIB = 1024 * 1024
LAG = 2

ROUTES = ((0, 0), (2, 4), (4, 2), (3, 5), (5, 3), (6, 6), (7, 7), (1, 1))

SMEM_SPEC = pl.BlockSpec(memory_space=pltpu.SMEM)
ANY_SPEC = pl.BlockSpec(memory_space=pl.ANY)
VMEM_SPEC = pl.BlockSpec(memory_space=pltpu.VMEM)


def routes(n_seq):
    return ROUTES if n_seq == 8 else tuple((k, k) for k in range(n_seq))


def back(n_seq, slot):
    first, second = routes(n_seq)[slot]
    return routes(n_seq).index((second, first) if first & 1 else (first, second))


def target(index_ref, n_seq, slot):
    first, second = routes(n_seq)[slot]
    own = index_ref[0]
    return own ^ (first + (second - first) * (own & 1))


def source(index_ref, n_seq, slot):
    return target(index_ref, n_seq, back(n_seq, slot))


def of_head(head):
    return pl.ds(pl.multiple_of(head * HEAD, HEAD), HEAD)


def token_specs(after):
    return [ANY_SPEC] * len(after)


def project_kernel(n_seq, at, beside, index_ref, tokens_ref, weight_ref, *refs):
    product, outs = refs[-1], refs[-1 - n_seq : -1]
    grad_ref = refs[0] if beside else None
    rows, depth = tokens_ref.shape
    heads = UNIT // HEAD

    def run(*sums):
        def body(block, carry):
            for deep in range(depth // UNIT):
                place = slice(deep * UNIT, (deep + 1) * UNIT)
                for unit in range(2):
                    columns = pl.ds(pl.multiple_of((block * 2 + unit) * UNIT, UNIT), UNIT)
                    pltpu.matmul_push_rhs(weight_ref[place, columns], deep % 2, unit)
                    pltpu.matmul_acc_lhs(sums[unit], tokens_ref[:, place], load_staged_rhs=deep % 2)
            for unit in range(2):
                done = pltpu.matmul_pop(sums[unit]).astype(jnp.bfloat16)
                for half in range(heads):
                    product[(block * 2 + unit) * heads + half] = done[:, half * HEAD : (half + 1) * HEAD]
            return carry

        lax.fori_loop(0, weight_ref.shape[1] // (2 * UNIT), body, 0)

    pl.run_scoped(run, *(pltpu.ACC(unit)((rows, UNIT), jnp.float32) for unit in range(2)))

    for slot in range(n_seq):
        head = target(index_ref, n_seq, slot)
        outs[slot][at] = product[head]
        if grad_ref is not None:
            outs[slot][1 - at] = grad_ref[:, of_head(head)]


def project(index, tokens, weight, at, grad_out=None, blocks=(), after=()):
    rows, depth = tokens.shape
    width = weight.shape[1]
    n_seq = width // HEAD
    extra = list(blocks) if grad_out is None else [grad_out]
    specs = [VMEM_SPEC] * len(extra) + token_specs(after)
    return pl.pallas_call(
        functools.partial(project_kernel, n_seq, at, grad_out is not None),
        in_specs=[SMEM_SPEC] + [VMEM_SPEC] * 2 + specs,
        out_specs=[VMEM_SPEC] * n_seq,
        out_shape=[jax.ShapeDtypeStruct((2, rows, HEAD), jnp.bfloat16)] * n_seq,
        input_output_aliases={3 + slot: slot for slot in range(len(blocks))},
        scratch_shapes=[pltpu.VMEM((n_seq, rows, HEAD), jnp.bfloat16)],
        compiler_params=pltpu.CompilerParams(vmem_limit_bytes=4 * MIB),
        cost_estimate=pl.CostEstimate(
            flops=2 * rows * depth * width, bytes_accessed=2 * depth * (rows + width), transcendentals=0
        ),
    )(index, tokens, weight, *extra, *after)


def hold_kernel(*refs):
    pass


def hold(blocks, after):
    count = len(blocks)
    return pl.pallas_call(
        hold_kernel,
        in_specs=[ANY_SPEC] * count + token_specs(after),
        out_specs=[ANY_SPEC] * count,
        out_shape=[jax.ShapeDtypeStruct(block.shape, block.dtype) for block in blocks],
        input_output_aliases={at: at for at in range(count)},
        compiler_params=pltpu.CompilerParams(vmem_limit_bytes=MIB),
    )(*blocks, *after)


def fold(block, reduce):
    return reduce(block.reshape(-1, 8, block.shape[1]), axis=0)


def attend_kernel(n_seq, low, high, total_rows, index_ref, *refs):
    tile = n_seq * SPAN
    begins = high == total_rows
    refs = list(refs)

    def take(count):
        taken = refs[:count]
        del refs[:count]
        return taken

    pairs, queries = take(n_seq), take(n_seq)
    carried = [] if begins else take(1)
    outs = take(n_seq)
    handed = take(1) if low else []
    pair, keys_t, scores, slopes, grad_pair, query, cotangent, bias = refs

    n_tiles = high // SPAN
    for at in range(n_tiles):
        for slot in range(n_seq):
            place = pl.ds(at * tile + slot * SPAN, SPAN)
            rows = pl.ds(at * SPAN, SPAN)
            pair[place, :HEAD] = pairs[slot][0, rows]
            pair[place, HEAD:] = pairs[slot][1, rows]
        keys_t[:, at * tile : (at + 1) * tile] = pair[at * tile : (at + 1) * tile, :HEAD].T

    def times(axis):
        row = lax.broadcasted_iota(jnp.int32, (tile, tile), axis)
        device = jnp.zeros((tile, tile), jnp.int32)
        for slot in range(n_seq):
            device = jnp.where(row // SPAN == slot, source(index_ref, n_seq, slot), device)
        return (row & (SPAN - 1)) * n_seq + device

    bias[...] = jnp.where(times(0) <= times(1), 0.0, LOW)
    scale = HEAD ** (-0.5)
    to_exp2 = scale * math.log2(math.e)
    blank = jnp.zeros((tile, HEAD), jnp.bfloat16)
    query[0, :, HEAD:] = blank
    query[1, :, :HEAD] = blank
    cotangent[0, :, HEAD:] = blank
    cotangent[1, :, :HEAD] = blank
    units = range(2)

    def span(base, half):
        return pl.ds(base + half * UNIT, UNIT)

    def columns(unit):
        return slice(unit * UNIT, (unit + 1) * UNIT)

    def run(sums, sums_query):
        def load(side):
            for unit in units:
                pltpu.matmul_push_rhs(side[columns(unit)], 0, unit, transpose=True)

        def stream(base, half, staged=None):
            for unit in units:
                pltpu.matmul_acc_lhs(sums[half][unit], pair[span(base, half)], load_staged_rhs=staged)

        def sweep(stripe, body, state):
            diagonal = stripe * tile

            def finish(base, half, state, shift=None):
                products = [pltpu.matmul_pop(sums[half][unit]) for unit in units]
                return body(base, half, products, state, shift)

            stream(diagonal, 0, 0)
            stream(diagonal, 1)
            state = finish(diagonal, 0, state, bias)
            if stripe:
                stream(0, 0)
            state = finish(diagonal, 1, state, bias)

            def step(i, state):
                base = pl.multiple_of(i * tile, tile)
                stream(base, 1)
                state = finish(base, 0, state)
                stream(pl.multiple_of(jnp.minimum(i + 1, stripe - 1) * tile, tile), 0)
                return finish(base, 1, state)

            if stripe:
                state = lax.fori_loop(0, stripe, step, state)
                for unit in units:
                    pltpu.matmul_pop(sums[0][unit])
            return state

        for stripe in range(n_tiles - 1, low // SPAN - 1, -1):
            offset = stripe * SPAN - low
            for slot in range(n_seq):
                place = pl.ds(slot * SPAN, SPAN)
                rows = slice(stripe * SPAN, (stripe + 1) * SPAN)
                query[0, place, :HEAD] = queries[slot][0, rows]
                query[1, place, HEAD:] = queries[slot][0, rows]
                cotangent[0, place, :HEAD] = queries[slot][1, rows]
                cotangent[1, place, HEAD:] = queries[slot][1, rows]
            diagonal = stripe * tile
            fresh = begins and stripe == n_tiles - 1

            def score(base, half, products, tops, shift):
                new = []
                for unit in units:
                    block = products[unit]
                    if shift is not None:
                        block = block + shift[half * UNIT : (half + 1) * UNIT, columns(unit)]
                    scores[span(base, half), columns(unit)] = block
                    new.append(jnp.maximum(tops[unit], fold(block, jnp.max)))
                return new

            load(query[0])
            tops = sweep(stripe, score, [jnp.full((8, UNIT), LOW, jnp.float32) for unit in units])
            tops = [jnp.max(top, axis=0, keepdims=True) for top in tops]

            def gauge(base, half, products, state, shift):
                new = []
                for unit in units:
                    total, dot = state[unit]
                    place = (span(base, half), columns(unit))
                    weights = jnp.exp2((scores[place] - tops[unit]) * to_exp2)
                    slopes[place] = products[unit]
                    new.append(
                        (total + fold(weights, jnp.sum), dot + fold(weights * products[unit], jnp.sum))
                    )
                return new

            load(cotangent[1])
            zeros = jnp.zeros((8, UNIT), jnp.float32)
            state = sweep(stripe, gauge, [(zeros, zeros) for unit in units])
            logsums, deltas = [], []
            for unit in units:
                total, dot = (jnp.sum(part, axis=0, keepdims=True) for part in state[unit])
                deltas.append(dot / total)
                logsums.append(tops[unit] + jnp.log2(total) * (1.0 / to_exp2))

            def grow(base):
                halves = range(2)
                probs, grads = {}, {}
                for half in halves:
                    for unit in units:
                        place = (span(base, half), columns(unit))
                        prob = jnp.exp2((scores[place] - logsums[unit]) * to_exp2)
                        grad = prob * (slopes[place] - deltas[unit])
                        probs[half, unit] = prob.astype(jnp.bfloat16)
                        grads[half, unit] = grad.astype(jnp.bfloat16)
                for unit in units:
                    pltpu.matmul_push_rhs(cotangent[0, columns(unit)], 0, unit)
                    pltpu.matmul_push_rhs(query[1, columns(unit)], 1, unit)
                for half in halves:
                    for unit in units:
                        pltpu.matmul_acc_lhs(
                            sums[half][unit], probs[half, unit], load_staged_rhs=None if half else 0
                        )
                for half in halves:
                    for unit in units:
                        pltpu.matmul_acc_lhs(
                            sums[half][unit], grads[half, unit], load_staged_rhs=None if half else 1
                        )
                for half in halves:
                    for unit in units:
                        pltpu.matmul_push_rhs(grads[half, unit], half, unit)
                        pltpu.matmul_acc_lhs(
                            sums_query[unit], keys_t[:, span(base, half)], load_staged_rhs=half
                        )
                for half in halves:
                    place = span(base, half)
                    part = pltpu.matmul_pop(sums[half][0]) + pltpu.matmul_pop(sums[half][1])
                    if fresh:
                        grad_pair[place] = part
                    elif stripe == n_tiles - 1:
                        grad_pair[place] = part + carried[0][place]
                    else:
                        grad_pair[place] += part

            grow(diagonal)
            if stripe:

                def step(i, carry):
                    grow(pl.multiple_of(i * tile, tile))
                    return carry

                lax.fori_loop(0, stripe, step, 0)

            for unit in units:
                done = (pltpu.matmul_pop(sums_query[unit]).T * scale).astype(jnp.bfloat16)
                for at in range(UNIT // SPAN):
                    slot = unit * (UNIT // SPAN) + at
                    outs[back(n_seq, slot)][0, offset : offset + SPAN] = done[
                        at * SPAN : (at + 1) * SPAN
                    ]
            for slot in range(n_seq):
                rows = pl.ds(diagonal + slot * SPAN, SPAN)
                place = slice(offset, offset + SPAN)
                out = outs[back(n_seq, slot)]
                out[1, place] = (grad_pair[rows, HEAD:] * scale).astype(jnp.bfloat16)
                out[2, place] = grad_pair[rows, :HEAD].astype(jnp.bfloat16)

    def accumulator(unit, rows):
        return pltpu.ACC(unit)((rows, UNIT), jnp.float32)

    pl.run_scoped(
        lambda a, b, c, d, e, f: run(((a, b), (c, d)), (e, f)),
        *(accumulator(unit, UNIT) for half in range(2) for unit in units),
        *(accumulator(unit, HEAD) for unit in units),
    )

    if low:
        handed[0][...] = grad_pair[: low * n_seq]


def attend(index, pairs, queries, carried, low, high):
    n_seq = len(pairs)
    total_rows = pairs[0].shape[1]
    tile = n_seq * SPAN
    depth = high * n_seq
    done = [jax.ShapeDtypeStruct((3, high - low, HEAD), jnp.bfloat16)] * n_seq
    handed = [jax.ShapeDtypeStruct((low * n_seq, 2 * HEAD), jnp.float32)] * (1 if low else 0)
    scratch = depth * (3 * 2 * HEAD + 4 * 2 * (tile + HEAD)) + tile * (2 * 8 * HEAD + 4 * tile)
    visible = (high * high - low * low) * n_seq * n_seq // 2
    results = pl.pallas_call(
        functools.partial(attend_kernel, n_seq, low, high, total_rows),
        in_specs=[SMEM_SPEC] + [VMEM_SPEC] * (2 * n_seq + len(carried)),
        out_specs=[VMEM_SPEC] * (n_seq + len(handed)),
        out_shape=done + handed,
        scratch_shapes=[
            pltpu.VMEM((depth, 2 * HEAD), jnp.bfloat16),
            pltpu.VMEM((HEAD, depth), jnp.bfloat16),
            pltpu.VMEM((depth, tile), jnp.float32),
            pltpu.VMEM((depth, tile), jnp.float32),
            pltpu.VMEM((depth, 2 * HEAD), jnp.float32),
            pltpu.VMEM((2, tile, 2 * HEAD), jnp.bfloat16),
            pltpu.VMEM((2, tile, 2 * HEAD), jnp.bfloat16),
            pltpu.VMEM((tile, tile), jnp.float32),
        ],
        compiler_params=pltpu.CompilerParams(vmem_limit_bytes=scratch + 3 * MIB),
        cost_estimate=pl.CostEstimate(
            flops=20 * HEAD * visible, bytes_accessed=8 * depth * HEAD, transcendentals=visible
        ),
    )(index, *pairs, *queries, *carried)
    return results[:n_seq], results[n_seq:]


def output_kernel(n_seq, base, index_ref, *refs):
    blocks, weights, (out_ref, joined, turned) = refs[:n_seq], refs[n_seq : n_seq + 3], refs[-3:]
    rows, width = blocks[0].shape[1], joined.shape[2]
    piece_rows, piece_columns = out_ref.shape
    groups = rows // piece_rows
    columns = piece_columns // groups
    half = columns // 2
    for slot in range(n_seq):
        place = of_head(source(index_ref, n_seq, slot))
        for at in range(3):
            joined[at, :rows, place] = blocks[slot][at]
    if rows < UNIT:
        joined[:, rows:] = jnp.zeros((3, UNIT - rows, width), jnp.bfloat16)
    for at in range(3):
        turned[at] = joined[at].T

    def run(*sums):
        for at in range(3):
            for part in range(width // UNIT):
                depth = slice(part * UNIT, (part + 1) * UNIT)
                staged = (at * (width // UNIT) + part) % 2
                for unit in range(2):
                    first = base + unit * half
                    pltpu.matmul_push_rhs(turned[at, depth], staged, unit)
                    pltpu.matmul_acc_lhs(
                        sums[unit], weights[at][first : first + half, depth], load_staged_rhs=staged
                    )
        for unit in range(2):
            total = pltpu.matmul_pop(sums[unit])[:, :rows].T.astype(jnp.bfloat16)
            for group in range(groups):
                first = group * columns + unit * half
                out_ref[:, first : first + half] = total[group * piece_rows : (group + 1) * piece_rows]

    pl.run_scoped(run, *(pltpu.ACC(unit)((half, UNIT), jnp.float32) for unit in range(2)))


def output_project(index, blocks, weights, piece, piece_rows, after=()):
    n_seq = len(blocks)
    rows = blocks[0].shape[1]
    depth, width = weights[0].shape
    columns = PIECE * piece_rows // rows
    return pl.pallas_call(
        functools.partial(output_kernel, n_seq, piece * columns),
        in_specs=[SMEM_SPEC] + [VMEM_SPEC] * (n_seq + 3) + token_specs(after),
        out_specs=VMEM_SPEC,
        out_shape=jax.ShapeDtypeStruct((piece_rows, PIECE), jnp.bfloat16),
        scratch_shapes=[
            pltpu.VMEM((3, UNIT, width), jnp.bfloat16),
            pltpu.VMEM((3, width, UNIT), jnp.bfloat16),
        ],
        compiler_params=pltpu.CompilerParams(vmem_limit_bytes=8 * MIB),
        cost_estimate=pl.CostEstimate(
            flops=6 * rows * columns * width, bytes_accessed=6 * columns * width, transcendentals=0
        ),
    )(index, *blocks, *weights, *after)


def trade(blocks):
    n_seq = len(blocks)
    arrived = [blocks[0]]
    for slot in range(1, n_seq):
        way = routes(n_seq)[slot]
        arrived.append(lax.ppermute(blocks[slot], "seq", [(i, i ^ way[i & 1]) for i in range(n_seq)]))
    return arrived


def relay_kernel(names, places, inner_ref, *refs):
    at = dict(zip(names, refs))

    def add(left, right):
        total = at[left][...].astype(jnp.float32) + at[right][...].astype(jnp.float32)
        return total.astype(jnp.bfloat16)

    if places:
        held, sem = refs[-2:]

        @pl.when(inner_ref[0] == 1)
        def kept():
            held[...] = at["sent"][...]

        @pl.when(inner_ref[0] == 0)
        def received():
            held[...] = at["arrived"][...]

        copies = []
        for group, (row, column, columns) in enumerate(places):
            rows = held.shape[0]
            copies.append(
                pltpu.make_async_copy(
                    held.at[:, group * columns : (group + 1) * columns],
                    at["result_out"].at[row : row + rows, column : column + columns],
                    sem.at[group],
                )
            )
            copies[-1].start()

    if "pair_out" in at:
        at["pair_out"][...] = add("part", "arrived")
    if "send_out" in at:

        @pl.when(inner_ref[0] == 1)
        def middle():
            at["send_out"][...] = add("pair", "crossed")

        if "fresh" in at:

            @pl.when(inner_ref[0] == 0)
            def outer():
                at["send_out"][...] = at["fresh"][...]

    if places:
        for copy in copies:
            copy.wait()


def relay(inner, inputs, outputs, places, result, result_shape, after=()):
    inputs = {name: value for name, value in inputs.items() if value is not None}
    shape = jax.ShapeDtypeStruct(next(iter(inputs.values())).shape, jnp.bfloat16)
    in_specs, out_specs, out_shape = [VMEM_SPEC] * len(inputs), [VMEM_SPEC] * len(outputs), [shape] * len(outputs)
    outputs = list(outputs)
    scratch, aliases, names = [], {}, list(inputs)
    unused = [str(at) for at in range(len(after))]
    operands = list(inputs.values())
    if places:
        if result is not None:
            aliases[1 + len(operands)] = len(outputs)
            operands.append(result)
            names.append("result")
            in_specs.append(ANY_SPEC)
        outputs.append("result_out")
        out_specs.append(ANY_SPEC)
        out_shape.append(jax.ShapeDtypeStruct(result_shape, jnp.bfloat16))
        scratch = [pltpu.VMEM(shape.shape, jnp.bfloat16), pltpu.SemaphoreType.DMA((len(places),))]
    results = pl.pallas_call(
        functools.partial(relay_kernel, names + unused + outputs, places),
        in_specs=[SMEM_SPEC] + in_specs + token_specs(after),
        out_specs=out_specs,
        out_shape=out_shape,
        input_output_aliases=aliases,
        scratch_shapes=scratch,
        compiler_params=pltpu.CompilerParams(vmem_limit_bytes=4 * MIB),
        cost_estimate=pl.CostEstimate(
            flops=2 * shape.size, bytes_accessed=4 * shape.size, transcendentals=0
        ),
    )(inner, *operands, *after)
    return dict(zip(outputs, results))


class LineSum:
    def __init__(self, inner, count, result_shape):
        self.inner, self.count, self.result_shape = inner, count, result_shape
        self.parts, self.places, self.sent, self.arrived = [], [], [], []
        self.pairs, self.crossed, self.result = {}, {}, None

    def relay(self, inputs, outputs, done=(), after=()):
        made = relay(self.inner, inputs, outputs, done, self.result, self.result_shape, after)
        self.result = made.get("result_out", self.result)
        return made

    def send(self, array, inward, outward):
        route = ([(0, 1), (3, 2)] if inward else []) + ([(1, 0), (2, 3)] if outward else [])
        self.sent.append(array)
        self.arrived.append(lax.ppermute(array, "tp", route))

    def cross(self, piece, pair):
        self.pairs[piece] = pair
        self.crossed[piece] = lax.ppermute(pair, "tp", [(1, 2), (2, 1)])

    def step(self, part, places):
        at = len(self.sent)
        self.parts.append(part)
        self.places.append(places)
        back = at - LAG
        inputs, outputs, done = {"arrived": self.arrived[back] if back >= 0 else None}, [], ()
        if back >= 0:
            inputs["part"] = self.parts[back]
            outputs.append("pair_out")
        if back >= LAG:
            inputs["pair"], inputs["crossed"] = self.pairs[back - LAG], self.crossed[back - LAG]
            inputs["fresh"] = part
            outputs.append("send_out")
        if back >= 2 * LAG:
            inputs["sent"] = self.sent[back]
            done = self.places[back - 2 * LAG]
        made = self.relay(inputs, outputs, done) if outputs else {}
        self.send(made.get("send_out", part), True, "send_out" in made)
        if "pair_out" in made:
            self.cross(back, made["pair_out"])
        return next(iter(made.values()), part)

    def finish(self):
        count = self.count
        token = []

        def outward(piece, after):
            inputs = {"pair": self.pairs[piece], "crossed": self.crossed[piece]}
            made = self.relay(inputs, ["send_out"], after=after)["send_out"]
            self.send(made, False, True)
            return [made]

        def inward(piece, after):
            inputs = {"arrived": self.arrived[piece], "part": self.parts[piece]}
            made = self.relay(inputs, ["pair_out"], after=after)["pair_out"]
            self.cross(piece, made)
            return [made]

        for piece in range(count - LAG, count):
            token = outward(piece - LAG, token)
            token = inward(piece, token)
        for piece in range(count - LAG, count):
            token = outward(piece, token + [self.arrived[piece + LAG]])
        for piece in range(count - 3 * LAG, count):
            at = piece + 2 * LAG
            inputs = {"arrived": self.arrived[at], "sent": self.sent[at]}
            self.relay(inputs, [], self.places[piece], token)
        return self.result


def swapped_shards(tokens, w_query, w_key, w_value, grad_out):
    rows, depth = tokens.shape
    n_seq = lax.axis_size("seq")
    tp = lax.axis_index("tp")
    inner = ((tp == 1) | (tp == 2)).astype(jnp.int32).reshape(1)
    index = lax.axis_index("seq").astype(jnp.int32).reshape(1)
    cut = rows // CHUNKS
    bounds = [(rows - cut, rows), (0, rows - cut)]

    queries = trade(project(index, tokens, w_query, 0, grad_out=grad_out, after=[inner]))
    pairs = project(index, tokens, w_key, 0, after=[queries[2]])
    pairs = trade(project(index, tokens, w_value, 1, blocks=pairs))

    line = LineSum(inner, CHUNKS * depth // PIECE, (rows, depth))
    weights = (w_query, w_key, w_value)

    def place(low, high, piece):
        groups = (high - low) // cut
        columns = PIECE // groups
        return [(low + group * cut, piece * columns, columns) for group in range(groups)]

    done, carried = attend(index, pairs, queries, [], *bounds[0])
    first = trade(done)
    done, carried = attend(index, pairs, queries, carried, *bounds[1])
    after = done[:1]
    for piece in range(depth // PIECE):
        part = output_project(index, first, weights, piece, cut, after)
        after = [line.step(part, place(*bounds[0], piece))]
        if piece == 1:
            second = trade(hold(done, after))
    for piece in range((CHUNKS - 1) * depth // PIECE):
        part = output_project(index, second, weights, piece, cut, after)
        after = [line.step(part, place(*bounds[1], piece))]
    return line.finish()


def shifted(block, axis, distance):
    devices = range(lax.axis_size(axis))
    route = [((i - distance) % len(devices), i) for i in devices]
    return lax.ppermute(block, axis, route)


def ring_shards(tokens, w_query, w_key, w_value, grad_out):
    rows = tokens.shape[0]
    local_heads = w_query.shape[1] // HEAD
    score_scale = HEAD ** (-0.5)
    cycle_size = lax.axis_size("seq")
    own_index = lax.axis_index("seq")

    def project(weight):
        product = jnp.dot(tokens, weight, preferred_element_type=jnp.float32).astype(jnp.bfloat16)
        return product.reshape(rows, local_heads, HEAD)

    queries = project(w_query)
    paired = jnp.stack((project(w_key), project(w_value)))
    grad_heads = grad_out.reshape(rows, local_heads, HEAD)
    offsets = jnp.arange(rows, dtype=jnp.int32) * cycle_size
    query_times = offsets + own_index

    def block_scores(key_block, source):
        scores = (
            jnp.einsum("qhd,khd->hqk", queries, key_block, preferred_element_type=jnp.float32)
            * score_scale
        )
        allowed = (offsets + source)[None, :] <= query_times[:, None]
        return jnp.where(allowed[None], scores, -1e30)

    def forward_step(running, pair, source):
        top, total, summed = running
        scores = block_scores(pair[0], source)
        new_top = jnp.maximum(top, jnp.max(scores, axis=2))
        factor = jnp.exp(top - new_top)
        weights = jnp.exp(scores - new_top[..., None])
        total = total * factor + jnp.sum(weights, axis=2)
        update = jnp.einsum(
            "hqk,khd->hqd",
            weights.astype(jnp.bfloat16),
            pair[1],
            preferred_element_type=jnp.float32,
        )
        summed = summed * factor[..., None] + update
        return (new_top, total, summed)

    start_state = (
        jnp.full((local_heads, rows), -1e30, jnp.float32),
        jnp.zeros((local_heads, rows), jnp.float32),
        jnp.zeros((local_heads, rows, HEAD), jnp.float32),
    )

    def cycle_forward(step, carry):
        pair, running = carry
        pair = shifted(pair, "seq", 1)
        source = (own_index - step) % cycle_size
        return (pair, forward_step(running, pair, source))

    first = forward_step(start_state, paired, own_index)
    unused, running = lax.fori_loop(1, cycle_size, cycle_forward, (paired, first))
    top, total, summed = running
    logsum = top + jnp.log(total)
    attended = (summed / total[..., None]).astype(jnp.bfloat16)
    row_delta = jnp.sum(
        grad_heads.astype(jnp.float32) * jnp.transpose(attended, (1, 0, 2)).astype(jnp.float32),
        axis=2,
    ).T

    def backward_step(pair, source):
        key_block = pair[0]
        value_block = pair[1]
        scores = block_scores(key_block, source)
        probs = jnp.exp(scores - logsum[..., None])
        grad_value = jnp.einsum(
            "hqk,qhd->khd",
            probs.astype(jnp.bfloat16),
            grad_heads,
            preferred_element_type=jnp.float32,
        )
        grad_probs = jnp.einsum(
            "qhd,khd->hqk", grad_heads, value_block, preferred_element_type=jnp.float32
        )
        grad_scores = (probs * (grad_probs - row_delta[..., None])).astype(jnp.bfloat16)
        grad_query = jnp.einsum(
            "hqk,khd->qhd", grad_scores, key_block, preferred_element_type=jnp.float32
        )
        grad_key = jnp.einsum(
            "hqk,qhd->khd", grad_scores, queries, preferred_element_type=jnp.float32
        )
        return (grad_query, jnp.stack((grad_key, grad_value)))

    query_zero = jnp.zeros((rows, local_heads, HEAD), jnp.float32)

    def cycle_backward(step, carry):
        pair, grad_query, grad_pair = carry
        source = (own_index - step) % cycle_size
        part_query, part_pair = backward_step(pair, source)
        pair = shifted(pair, "seq", 1)
        grad_pair = shifted((grad_pair + part_pair).astype(jnp.bfloat16), "seq", 1).astype(
            jnp.float32
        )
        return (pair, grad_query + part_query, grad_pair)

    pair_zero = jnp.zeros((2, rows, local_heads, HEAD), jnp.float32)
    pair, grad_query, grad_pair = lax.fori_loop(
        0, cycle_size - 1, cycle_backward, (paired, query_zero, pair_zero)
    )
    last_source = (own_index + 1) % cycle_size
    part_query, part_pair = backward_step(pair, last_source)
    grad_query = grad_query + part_query
    grad_pair = shifted((grad_pair + part_pair).astype(jnp.bfloat16), "seq", 1).astype(jnp.float32)
    width = local_heads * HEAD
    query_low = (grad_query * score_scale).astype(jnp.bfloat16).reshape(rows, width)
    key_low = (grad_pair[0] * score_scale).astype(jnp.bfloat16).reshape(rows, width)
    value_low = grad_pair[1].astype(jnp.bfloat16).reshape(rows, width)
    partial_sum = jnp.dot(query_low, w_query.T, preferred_element_type=jnp.float32)
    partial_sum = partial_sum + jnp.dot(key_low, w_key.T, preferred_element_type=jnp.float32)
    partial_sum = partial_sum + jnp.dot(value_low, w_value.T, preferred_element_type=jnp.float32)
    return lax.psum(partial_sum.astype(jnp.bfloat16), "tp")


def solution(mesh):
    placed = (P("seq", None), P(None, "tp"), P(None, "tp"), P(None, "tp"), P("seq", "tp"))
    n_seq, n_tp = mesh.shape["seq"], mesh.shape["tp"]

    def shards(tokens, w_query, w_key, w_value, grad_out):
        fits = (
            w_query.shape[1] == n_seq * HEAD
            and n_seq & (n_seq - 1) == 0
            and n_tp == 4
            and tokens.shape[0] % (CHUNKS * SPAN) == 0
            and tokens.shape[1] % PIECE == 0
        )
        chosen = swapped_shards if fits else ring_shards
        return chosen(tokens, w_query, w_key, w_value, grad_out)

    return jax.shard_map(
        shards, mesh=mesh, in_specs=placed, out_specs=P("seq", None), check_vma=False
    )
```

```python
import functools
import math

import jax
import jax.numpy as jnp
from jax import lax
from jax.experimental import pallas as pl
from jax.experimental.pallas import tpu as pltpu
from jax.sharding import PartitionSpec as P

HEAD = 128
SPAN = 64
CHUNKS = 3
PIECE = 1024
UNIT = 256
LOW = -1e30
MIB = 1024 * 1024
LAG = 2

ROUTES = ((0, 0), (2, 4), (4, 2), (3, 5), (5, 3), (6, 6), (7, 7), (1, 1))

SMEM_SPEC = pl.BlockSpec(memory_space=pltpu.SMEM)
ANY_SPEC = pl.BlockSpec(memory_space=pl.ANY)
VMEM_SPEC = pl.BlockSpec(memory_space=pltpu.VMEM)


def routes(n_seq):
    return ROUTES if n_seq == 8 else tuple((k, k) for k in range(n_seq))


def back(n_seq, slot):
    first, second = routes(n_seq)[slot]
    return routes(n_seq).index((second, first) if first & 1 else (first, second))


def target(index_ref, n_seq, slot):
    first, second = routes(n_seq)[slot]
    own = index_ref[0]
    return own ^ (first + (second - first) * (own & 1))


def source(index_ref, n_seq, slot):
    return target(index_ref, n_seq, back(n_seq, slot))


def of_head(head):
    return pl.ds(pl.multiple_of(head * HEAD, HEAD), HEAD)


def token_specs(after):
    return [ANY_SPEC] * len(after)


def project_kernel(n_seq, at, beside, index_ref, tokens_ref, weight_ref, *refs):
    product, outs = refs[-1], refs[-1 - n_seq : -1]
    grad_ref = refs[0] if beside else None
    rows, depth = tokens_ref.shape
    heads = UNIT // HEAD

    def run(*sums):
        def body(block, carry):
            for deep in range(depth // UNIT):
                place = slice(deep * UNIT, (deep + 1) * UNIT)
                for unit in range(2):
                    columns = pl.ds(pl.multiple_of((block * 2 + unit) * UNIT, UNIT), UNIT)
                    pltpu.matmul_push_rhs(weight_ref[place, columns], deep % 2, unit)
                    pltpu.matmul_acc_lhs(sums[unit], tokens_ref[:, place], load_staged_rhs=deep % 2)
            for unit in range(2):
                done = pltpu.matmul_pop(sums[unit]).astype(jnp.bfloat16)
                for half in range(heads):
                    product[(block * 2 + unit) * heads + half] = done[:, half * HEAD : (half + 1) * HEAD]
            return carry

        lax.fori_loop(0, weight_ref.shape[1] // (2 * UNIT), body, 0)

    pl.run_scoped(run, *(pltpu.ACC(unit)((rows, UNIT), jnp.float32) for unit in range(2)))

    for slot in range(n_seq):
        head = target(index_ref, n_seq, slot)
        outs[slot][at] = product[head]
        if grad_ref is not None:
            outs[slot][1 - at] = grad_ref[:, of_head(head)]


def project(index, tokens, weight, at, grad_out=None, blocks=(), after=()):
    rows, depth = tokens.shape
    width = weight.shape[1]
    n_seq = width // HEAD
    extra = list(blocks) if grad_out is None else [grad_out]
    specs = [VMEM_SPEC] * len(extra) + token_specs(after)
    return pl.pallas_call(
        functools.partial(project_kernel, n_seq, at, grad_out is not None),
        in_specs=[SMEM_SPEC] + [VMEM_SPEC] * 2 + specs,
        out_specs=[VMEM_SPEC] * n_seq,
        out_shape=[jax.ShapeDtypeStruct((2, rows, HEAD), jnp.bfloat16)] * n_seq,
        input_output_aliases={3 + slot: slot for slot in range(len(blocks))},
        scratch_shapes=[pltpu.VMEM((n_seq, rows, HEAD), jnp.bfloat16)],
        compiler_params=pltpu.CompilerParams(vmem_limit_bytes=4 * MIB),
        cost_estimate=pl.CostEstimate(
            flops=2 * rows * depth * width, bytes_accessed=2 * depth * (rows + width), transcendentals=0
        ),
    )(index, tokens, weight, *extra, *after)


def hold_kernel(*refs):
    pass


def hold(blocks, after):
    count = len(blocks)
    return pl.pallas_call(
        hold_kernel,
        in_specs=[ANY_SPEC] * count + token_specs(after),
        out_specs=[ANY_SPEC] * count,
        out_shape=[jax.ShapeDtypeStruct(block.shape, block.dtype) for block in blocks],
        input_output_aliases={at: at for at in range(count)},
        compiler_params=pltpu.CompilerParams(vmem_limit_bytes=MIB),
    )(*blocks, *after)


def fold(block, reduce):
    return reduce(block.reshape(-1, 8, block.shape[1]), axis=0)


def attend_kernel(n_seq, low, high, total_rows, index_ref, *refs):
    tile = n_seq * SPAN
    begins = high == total_rows
    refs = list(refs)

    def take(count):
        taken = refs[:count]
        del refs[:count]
        return taken

    pairs, queries = take(n_seq), take(n_seq)
    carried = [] if begins else take(1)
    outs = take(n_seq)
    handed = take(1) if low else []
    pair, keys_t, scores, slopes, grad_pair, query, cotangent, bias = refs

    n_tiles = high // SPAN
    for at in range(n_tiles):
        for slot in range(n_seq):
            place = pl.ds(at * tile + slot * SPAN, SPAN)
            rows = pl.ds(at * SPAN, SPAN)
            pair[place, :HEAD] = pairs[slot][0, rows]
            pair[place, HEAD:] = pairs[slot][1, rows]
        keys_t[:, at * tile : (at + 1) * tile] = pair[at * tile : (at + 1) * tile, :HEAD].T

    def times(shape, axis):
        row = lax.broadcasted_iota(jnp.int32, shape, axis)
        device = jnp.zeros(shape, jnp.int32)
        for slot in range(n_seq):
            device = jnp.where(row // SPAN == slot, source(index_ref, n_seq, slot), device)
        return (row & (SPAN - 1)) * n_seq + device

    grad_pair[...] = carried[0][...] if carried else jnp.zeros(grad_pair.shape, jnp.float32)
    bias[...] = jnp.where(times((tile, HEAD), 0)[:, :1] <= times((8, tile), 1)[:1], 0.0, LOW)
    scale = HEAD ** (-0.5)
    blank = jnp.zeros((tile, HEAD), jnp.bfloat16)
    query[0, :, HEAD:] = blank
    query[1, :, :HEAD] = blank
    cotangent[0, :, HEAD:] = blank
    cotangent[1, :, :HEAD] = blank
    units = range(2)

    def span(base, half):
        return pl.ds(base + half * UNIT, UNIT)

    def columns(unit):
        return slice(unit * UNIT, (unit + 1) * UNIT)

    def run(sums, sums_query):
        def load(side):
            for unit in units:
                pltpu.matmul_push_rhs(side[columns(unit)], 0, unit, transpose=True)

        def stream(base, half, staged=None):
            for unit in units:
                pltpu.matmul_acc_lhs(sums[half][unit], pair[span(base, half)], load_staged_rhs=staged)

        def tile_at(at):
            return pl.multiple_of(at * tile, tile)

        def sweep(first, count, body, state):
            def finish(base, half, state, shift=None):
                products = [pltpu.matmul_pop(sums[half][unit]) for unit in units]
                return body(base, half, products, state, shift)

            if first is None:
                stream(0, 0, 0)
            else:
                stream(first, 0, 0)
                stream(first, 1)
                state = finish(first, 0, state, bias)
                stream(0, 0)
                state = finish(first, 1, state, bias)

            def step(at, state):
                base = tile_at(at)
                stream(base, 1)
                state = finish(base, 0, state)
                stream(tile_at(jnp.maximum(jnp.minimum(at + 1, count - 1), 0)), 0)
                return finish(base, 1, state)

            state = lax.fori_loop(0, count, step, state)
            for unit in units:
                pltpu.matmul_pop(sums[0][unit])
            return state

        def work(step, carry):
            stripe = n_tiles - 1 - step
            offset = pl.multiple_of(stripe * SPAN - low, SPAN)
            for slot in range(n_seq):
                place = pl.ds(slot * SPAN, SPAN)
                rows = pl.ds(pl.multiple_of(stripe * SPAN, SPAN), SPAN)
                query[0, place, :HEAD] = queries[slot][0, rows]
                query[1, place, HEAD:] = queries[slot][0, rows]
                cotangent[0, place, :HEAD] = queries[slot][1, rows]
                cotangent[1, place, HEAD:] = queries[slot][1, rows]
            diagonal = tile_at(stripe)

            def score(base, half, products, tops, shift):
                new = []
                for unit in units:
                    block = products[unit] * scale
                    if shift is not None:
                        block = block + shift[half * UNIT : (half + 1) * UNIT, columns(unit)]
                    scores[span(base, half), columns(unit)] = block
                    new.append(jnp.maximum(tops[unit], fold(block, jnp.max)))
                return new

            load(query[0])
            tops = sweep(diagonal, stripe, score, [jnp.full((8, UNIT), LOW, jnp.float32) for unit in units])
            tops = [jnp.max(top, axis=0, keepdims=True) for top in tops]

            def gauge(base, half, products, state, shift):
                new = []
                for unit in units:
                    total, dot = state[unit]
                    place = (span(base, half), columns(unit))
                    weights = jnp.exp(scores[place] - tops[unit])
                    slopes[place] = products[unit]
                    new.append(
                        (total + fold(weights, jnp.sum), dot + fold(weights * products[unit], jnp.sum))
                    )
                return new

            load(cotangent[1])
            zeros = jnp.zeros((8, UNIT), jnp.float32)
            state = sweep(None, stripe + 1, gauge, [(zeros, zeros) for unit in units])
            logsums, deltas = [], []
            for unit in units:
                total, dot = (jnp.sum(part, axis=0, keepdims=True) for part in state[unit])
                deltas.append(dot / total)
                logsums.append(tops[unit] + jnp.log(total))

            def grow(base):
                halves = range(2)
                probs = {}
                for unit in units:
                    pltpu.matmul_push_rhs(cotangent[0, columns(unit)], 0, unit)
                    pltpu.matmul_push_rhs(query[1, columns(unit)], 1, unit)
                for half in halves:
                    for unit in units:
                        prob = jnp.exp(scores[span(base, half), columns(unit)] - logsums[unit])
                        pltpu.matmul_acc_lhs(
                            sums[half][unit],
                            prob.astype(jnp.bfloat16),
                            load_staged_rhs=None if half else 0,
                        )
                        probs[half, unit] = prob
                for half in halves:
                    for unit in units:
                        slope = slopes[span(base, half), columns(unit)]
                        grad = (probs[half, unit] * (slope - deltas[unit])).astype(jnp.bfloat16)
                        if half == 0:
                            pltpu.matmul_push_rhs(grad, 0, unit)
                        pltpu.matmul_acc_lhs(sums[half][unit], grad, load_staged_rhs=None if half else 1)
                        if half == 1:
                            pltpu.matmul_push_rhs(grad, 1, unit)
                for half in halves:
                    for unit in units:
                        pltpu.matmul_acc_lhs(
                            sums_query[unit], keys_t[:, span(base, half)], load_staged_rhs=half
                        )
                for half in halves:
                    place = span(base, half)
                    part = pltpu.matmul_pop(sums[half][0]) + pltpu.matmul_pop(sums[half][1])
                    grad_pair[place] += part

            def grow_step(at, carry):
                grow(tile_at(at))
                return carry

            lax.fori_loop(0, stripe + 1, grow_step, 0)

            for unit in units:
                done = (pltpu.matmul_pop(sums_query[unit]).T * scale).astype(jnp.bfloat16)
                for at in range(UNIT // SPAN):
                    slot = unit * (UNIT // SPAN) + at
                    outs[back(n_seq, slot)][0, pl.ds(offset, SPAN)] = done[
                        at * SPAN : (at + 1) * SPAN
                    ]
            for slot in range(n_seq):
                rows = pl.ds(diagonal + slot * SPAN, SPAN)
                place = pl.ds(offset, SPAN)
                out = outs[back(n_seq, slot)]
                out[1, place] = (grad_pair[rows, HEAD:] * scale).astype(jnp.bfloat16)
                out[2, place] = grad_pair[rows, :HEAD].astype(jnp.bfloat16)
            return carry

        lax.fori_loop(0, n_tiles - low // SPAN, work, 0)

    def accumulator(unit, rows):
        return pltpu.ACC(unit)((rows, UNIT), jnp.float32)

    pl.run_scoped(
        lambda a, b, c, d, e, f: run(((a, b), (c, d)), (e, f)),
        *(accumulator(unit, UNIT) for half in range(2) for unit in units),
        *(accumulator(unit, HEAD) for unit in units),
    )

    if low:
        handed[0][...] = grad_pair[: low * n_seq]


def attend(index, pairs, queries, carried, low, high):
    n_seq = len(pairs)
    total_rows = pairs[0].shape[1]
    tile = n_seq * SPAN
    depth = high * n_seq
    done = [jax.ShapeDtypeStruct((3, high - low, HEAD), jnp.bfloat16)] * n_seq
    handed = [jax.ShapeDtypeStruct((low * n_seq, 2 * HEAD), jnp.float32)] * (1 if low else 0)
    scratch = depth * (3 * 2 * HEAD + 4 * 2 * (tile + HEAD)) + tile * (2 * 8 * HEAD + 4 * tile)
    visible = (high * high - low * low) * n_seq * n_seq // 2
    results = pl.pallas_call(
        functools.partial(attend_kernel, n_seq, low, high, total_rows),
        in_specs=[SMEM_SPEC] + [VMEM_SPEC] * (2 * n_seq + len(carried)),
        out_specs=[VMEM_SPEC] * (n_seq + len(handed)),
        out_shape=done + handed,
        scratch_shapes=[
            pltpu.VMEM((depth, 2 * HEAD), jnp.bfloat16),
            pltpu.VMEM((HEAD, depth), jnp.bfloat16),
            pltpu.VMEM((depth, tile), jnp.float32),
            pltpu.VMEM((depth, tile), jnp.float32),
            pltpu.VMEM((depth, 2 * HEAD), jnp.float32),
            pltpu.VMEM((2, tile, 2 * HEAD), jnp.bfloat16),
            pltpu.VMEM((2, tile, 2 * HEAD), jnp.bfloat16),
            pltpu.VMEM((tile, tile), jnp.float32),
        ],
        compiler_params=pltpu.CompilerParams(vmem_limit_bytes=scratch + 3 * MIB),
        cost_estimate=pl.CostEstimate(
            flops=20 * HEAD * visible, bytes_accessed=8 * depth * HEAD, transcendentals=visible
        ),
    )(index, *pairs, *queries, *carried)
    return results[:n_seq], results[n_seq:]


def output_kernel(n_seq, base, index_ref, *refs):
    blocks, weights, (out_ref, joined, turned) = refs[:n_seq], refs[n_seq : n_seq + 3], refs[-3:]
    rows, width = blocks[0].shape[1], joined.shape[2]
    piece_rows, piece_columns = out_ref.shape
    groups = rows // piece_rows
    columns = piece_columns // groups
    half = columns // 2
    for slot in range(n_seq):
        place = of_head(source(index_ref, n_seq, slot))
        for at in range(3):
            joined[at, :rows, place] = blocks[slot][at]
    if rows < UNIT:
        joined[:, rows:] = jnp.zeros((3, UNIT - rows, width), jnp.bfloat16)
    for at in range(3):
        turned[at] = joined[at].T

    def run(*sums):
        for at in range(3):
            for part in range(width // UNIT):
                depth = slice(part * UNIT, (part + 1) * UNIT)
                staged = (at * (width // UNIT) + part) % 2
                for unit in range(2):
                    first = base + unit * half
                    pltpu.matmul_push_rhs(turned[at, depth], staged, unit)
                    pltpu.matmul_acc_lhs(
                        sums[unit], weights[at][first : first + half, depth], load_staged_rhs=staged
                    )
        for unit in range(2):
            total = pltpu.matmul_pop(sums[unit])[:, :rows].T.astype(jnp.bfloat16)
            for group in range(groups):
                first = group * columns + unit * half
                out_ref[:, first : first + half] = total[group * piece_rows : (group + 1) * piece_rows]

    pl.run_scoped(run, *(pltpu.ACC(unit)((half, UNIT), jnp.float32) for unit in range(2)))


def output_project(index, blocks, weights, piece, piece_rows, after=()):
    n_seq = len(blocks)
    rows = blocks[0].shape[1]
    depth, width = weights[0].shape
    columns = PIECE * piece_rows // rows
    return pl.pallas_call(
        functools.partial(output_kernel, n_seq, piece * columns),
        in_specs=[SMEM_SPEC] + [VMEM_SPEC] * (n_seq + 3) + token_specs(after),
        out_specs=VMEM_SPEC,
        out_shape=jax.ShapeDtypeStruct((piece_rows, PIECE), jnp.bfloat16),
        scratch_shapes=[
            pltpu.VMEM((3, UNIT, width), jnp.bfloat16),
            pltpu.VMEM((3, width, UNIT), jnp.bfloat16),
        ],
        compiler_params=pltpu.CompilerParams(vmem_limit_bytes=8 * MIB),
        cost_estimate=pl.CostEstimate(
            flops=6 * rows * columns * width, bytes_accessed=6 * columns * width, transcendentals=0
        ),
    )(index, *blocks, *weights, *after)


def trade(blocks):
    n_seq = len(blocks)
    arrived = [blocks[0]]
    for slot in range(1, n_seq):
        way = routes(n_seq)[slot]
        arrived.append(lax.ppermute(blocks[slot], "seq", [(i, i ^ way[i & 1]) for i in range(n_seq)]))
    return arrived


def relay_kernel(names, places, inner_ref, *refs):
    at = dict(zip(names, refs))

    def add(left, right):
        total = at[left][...].astype(jnp.float32) + at[right][...].astype(jnp.float32)
        return total.astype(jnp.bfloat16)

    if places:
        held, sem = refs[-2:]

        @pl.when(inner_ref[0] == 1)
        def kept():
            held[...] = at["sent"][...]

        @pl.when(inner_ref[0] == 0)
        def received():
            held[...] = at["arrived"][...]

        copies = []
        for group, (row, column, columns) in enumerate(places):
            rows = held.shape[0]
            copies.append(
                pltpu.make_async_copy(
                    held.at[:, group * columns : (group + 1) * columns],
                    at["result_out"].at[row : row + rows, column : column + columns],
                    sem.at[group],
                )
            )
            copies[-1].start()

    if "pair_out" in at:
        at["pair_out"][...] = add("part", "arrived")
    if "send_out" in at:

        @pl.when(inner_ref[0] == 1)
        def middle():
            at["send_out"][...] = add("pair", "crossed")

        if "fresh" in at:

            @pl.when(inner_ref[0] == 0)
            def outer():
                at["send_out"][...] = at["fresh"][...]

    if places:
        for copy in copies:
            copy.wait()


def relay(inner, inputs, outputs, places, result, result_shape, after=()):
    inputs = {name: value for name, value in inputs.items() if value is not None}
    shape = jax.ShapeDtypeStruct(next(iter(inputs.values())).shape, jnp.bfloat16)
    in_specs, out_specs, out_shape = [VMEM_SPEC] * len(inputs), [VMEM_SPEC] * len(outputs), [shape] * len(outputs)
    outputs = list(outputs)
    scratch, aliases, names = [], {}, list(inputs)
    unused = [str(at) for at in range(len(after))]
    operands = list(inputs.values())
    if places:
        if result is not None:
            aliases[1 + len(operands)] = len(outputs)
            operands.append(result)
            names.append("result")
            in_specs.append(ANY_SPEC)
        outputs.append("result_out")
        out_specs.append(ANY_SPEC)
        out_shape.append(jax.ShapeDtypeStruct(result_shape, jnp.bfloat16))
        scratch = [pltpu.VMEM(shape.shape, jnp.bfloat16), pltpu.SemaphoreType.DMA((len(places),))]
    results = pl.pallas_call(
        functools.partial(relay_kernel, names + unused + outputs, places),
        in_specs=[SMEM_SPEC] + in_specs + token_specs(after),
        out_specs=out_specs,
        out_shape=out_shape,
        input_output_aliases=aliases,
        scratch_shapes=scratch,
        compiler_params=pltpu.CompilerParams(vmem_limit_bytes=4 * MIB),
        cost_estimate=pl.CostEstimate(
            flops=2 * shape.size, bytes_accessed=4 * shape.size, transcendentals=0
        ),
    )(inner, *operands, *after)
    return dict(zip(outputs, results))


class LineSum:
    def __init__(self, inner, count, result_shape):
        self.inner, self.count, self.result_shape = inner, count, result_shape
        self.parts, self.places, self.sent, self.arrived = [], [], [], []
        self.pairs, self.crossed, self.result = {}, {}, None

    def relay(self, inputs, outputs, done=(), after=()):
        made = relay(self.inner, inputs, outputs, done, self.result, self.result_shape, after)
        self.result = made.get("result_out", self.result)
        return made

    def send(self, array, inward, outward):
        route = ([(0, 1), (3, 2)] if inward else []) + ([(1, 0), (2, 3)] if outward else [])
        self.sent.append(array)
        self.arrived.append(lax.ppermute(array, "tp", route))

    def cross(self, piece, pair):
        self.pairs[piece] = pair
        self.crossed[piece] = lax.ppermute(pair, "tp", [(1, 2), (2, 1)])

    def step(self, part, places):
        at = len(self.sent)
        self.parts.append(part)
        self.places.append(places)
        back = at - LAG
        inputs, outputs, done = {"arrived": self.arrived[back] if back >= 0 else None}, [], ()
        if back >= 0:
            inputs["part"] = self.parts[back]
            outputs.append("pair_out")
        if back >= LAG:
            inputs["pair"], inputs["crossed"] = self.pairs[back - LAG], self.crossed[back - LAG]
            inputs["fresh"] = part
            outputs.append("send_out")
        if back >= 2 * LAG:
            inputs["sent"] = self.sent[back]
            done = self.places[back - 2 * LAG]
        made = self.relay(inputs, outputs, done) if outputs else {}
        self.send(made.get("send_out", part), True, "send_out" in made)
        if "pair_out" in made:
            self.cross(back, made["pair_out"])
        return next(iter(made.values()), part)

    def finish(self):
        count = self.count
        token = []

        def outward(piece, after):
            inputs = {"pair": self.pairs[piece], "crossed": self.crossed[piece]}
            made = self.relay(inputs, ["send_out"], after=after)["send_out"]
            self.send(made, False, True)
            return [made]

        def inward(piece, after):
            inputs = {"arrived": self.arrived[piece], "part": self.parts[piece]}
            made = self.relay(inputs, ["pair_out"], after=after)["pair_out"]
            self.cross(piece, made)
            return [made]

        for piece in range(count - LAG, count):
            token = outward(piece - LAG, token)
            token = inward(piece, token)
        for piece in range(count - LAG, count):
            token = outward(piece, token + [self.arrived[piece + LAG]])
        for piece in range(count - 3 * LAG, count):
            at = piece + 2 * LAG
            inputs = {"arrived": self.arrived[at], "sent": self.sent[at]}
            self.relay(inputs, [], self.places[piece], token)
        return self.result


def swapped_shards(tokens, w_query, w_key, w_value, grad_out):
    rows, depth = tokens.shape
    n_seq = lax.axis_size("seq")
    tp = lax.axis_index("tp")
    inner = ((tp == 1) | (tp == 2)).astype(jnp.int32).reshape(1)
    index = lax.axis_index("seq").astype(jnp.int32).reshape(1)
    cut = rows // CHUNKS
    bounds = [(rows - cut, rows), (0, rows - cut)]

    queries = trade(project(index, tokens, w_query, 0, grad_out=grad_out, after=[inner]))
    pairs = project(index, tokens, w_key, 0, after=[queries[2]])
    pairs = trade(project(index, tokens, w_value, 1, blocks=pairs))

    line = LineSum(inner, CHUNKS * depth // PIECE, (rows, depth))
    weights = (w_query, w_key, w_value)

    def place(low, high, piece):
        groups = (high - low) // cut
        columns = PIECE // groups
        return [(low + group * cut, piece * columns, columns) for group in range(groups)]

    done, carried = attend(index, pairs, queries, [], *bounds[0])
    first = trade(done)
    done, carried = attend(index, pairs, queries, carried, *bounds[1])
    after = done[:1]
    for piece in range(depth // PIECE):
        part = output_project(index, first, weights, piece, cut, after)
        after = [line.step(part, place(*bounds[0], piece))]
        if piece == 1:
            second = trade(hold(done, after))
    for piece in range((CHUNKS - 1) * depth // PIECE):
        part = output_project(index, second, weights, piece, cut, after)
        after = [line.step(part, place(*bounds[1], piece))]
    return line.finish()


def shifted(block, axis, distance):
    devices = range(lax.axis_size(axis))
    route = [((i - distance) % len(devices), i) for i in devices]
    return lax.ppermute(block, axis, route)


def ring_shards(tokens, w_query, w_key, w_value, grad_out):
    rows = tokens.shape[0]
    local_heads = w_query.shape[1] // HEAD
    score_scale = HEAD ** (-0.5)
    cycle_size = lax.axis_size("seq")
    own_index = lax.axis_index("seq")

    def project(weight):
        product = jnp.dot(tokens, weight, preferred_element_type=jnp.float32).astype(jnp.bfloat16)
        return product.reshape(rows, local_heads, HEAD)

    queries = project(w_query)
    paired = jnp.stack((project(w_key), project(w_value)))
    grad_heads = grad_out.reshape(rows, local_heads, HEAD)
    offsets = jnp.arange(rows, dtype=jnp.int32) * cycle_size
    query_times = offsets + own_index

    def block_scores(key_block, source):
        scores = (
            jnp.einsum("qhd,khd->hqk", queries, key_block, preferred_element_type=jnp.float32)
            * score_scale
        )
        allowed = (offsets + source)[None, :] <= query_times[:, None]
        return jnp.where(allowed[None], scores, -1e30)

    def forward_step(running, pair, source):
        top, total, summed = running
        scores = block_scores(pair[0], source)
        new_top = jnp.maximum(top, jnp.max(scores, axis=2))
        factor = jnp.exp(top - new_top)
        weights = jnp.exp(scores - new_top[..., None])
        total = total * factor + jnp.sum(weights, axis=2)
        update = jnp.einsum(
            "hqk,khd->hqd",
            weights.astype(jnp.bfloat16),
            pair[1],
            preferred_element_type=jnp.float32,
        )
        summed = summed * factor[..., None] + update
        return (new_top, total, summed)

    start_state = (
        jnp.full((local_heads, rows), -1e30, jnp.float32),
        jnp.zeros((local_heads, rows), jnp.float32),
        jnp.zeros((local_heads, rows, HEAD), jnp.float32),
    )

    def cycle_forward(step, carry):
        pair, running = carry
        pair = shifted(pair, "seq", 1)
        source = (own_index - step) % cycle_size
        return (pair, forward_step(running, pair, source))

    first = forward_step(start_state, paired, own_index)
    unused, running = lax.fori_loop(1, cycle_size, cycle_forward, (paired, first))
    top, total, summed = running
    logsum = top + jnp.log(total)
    attended = (summed / total[..., None]).astype(jnp.bfloat16)
    row_delta = jnp.sum(
        grad_heads.astype(jnp.float32) * jnp.transpose(attended, (1, 0, 2)).astype(jnp.float32),
        axis=2,
    ).T

    def backward_step(pair, source):
        key_block = pair[0]
        value_block = pair[1]
        scores = block_scores(key_block, source)
        probs = jnp.exp(scores - logsum[..., None])
        grad_value = jnp.einsum(
            "hqk,qhd->khd",
            probs.astype(jnp.bfloat16),
            grad_heads,
            preferred_element_type=jnp.float32,
        )
        grad_probs = jnp.einsum(
            "qhd,khd->hqk", grad_heads, value_block, preferred_element_type=jnp.float32
        )
        grad_scores = (probs * (grad_probs - row_delta[..., None])).astype(jnp.bfloat16)
        grad_query = jnp.einsum(
            "hqk,khd->qhd", grad_scores, key_block, preferred_element_type=jnp.float32
        )
        grad_key = jnp.einsum(
            "hqk,qhd->khd", grad_scores, queries, preferred_element_type=jnp.float32
        )
        return (grad_query, jnp.stack((grad_key, grad_value)))

    query_zero = jnp.zeros((rows, local_heads, HEAD), jnp.float32)

    def cycle_backward(step, carry):
        pair, grad_query, grad_pair = carry
        source = (own_index - step) % cycle_size
        part_query, part_pair = backward_step(pair, source)
        pair = shifted(pair, "seq", 1)
        grad_pair = shifted((grad_pair + part_pair).astype(jnp.bfloat16), "seq", 1).astype(
            jnp.float32
        )
        return (pair, grad_query + part_query, grad_pair)

    pair_zero = jnp.zeros((2, rows, local_heads, HEAD), jnp.float32)
    pair, grad_query, grad_pair = lax.fori_loop(
        0, cycle_size - 1, cycle_backward, (paired, query_zero, pair_zero)
    )
    last_source = (own_index + 1) % cycle_size
    part_query, part_pair = backward_step(pair, last_source)
    grad_query = grad_query + part_query
    grad_pair = shifted((grad_pair + part_pair).astype(jnp.bfloat16), "seq", 1).astype(jnp.float32)
    width = local_heads * HEAD
    query_low = (grad_query * score_scale).astype(jnp.bfloat16).reshape(rows, width)
    key_low = (grad_pair[0] * score_scale).astype(jnp.bfloat16).reshape(rows, width)
    value_low = grad_pair[1].astype(jnp.bfloat16).reshape(rows, width)
    partial_sum = jnp.dot(query_low, w_query.T, preferred_element_type=jnp.float32)
    partial_sum = partial_sum + jnp.dot(key_low, w_key.T, preferred_element_type=jnp.float32)
    partial_sum = partial_sum + jnp.dot(value_low, w_value.T, preferred_element_type=jnp.float32)
    return lax.psum(partial_sum.astype(jnp.bfloat16), "tp")


def solution(mesh):
    placed = (P("seq", None), P(None, "tp"), P(None, "tp"), P(None, "tp"), P("seq", "tp"))
    n_seq, n_tp = mesh.shape["seq"], mesh.shape["tp"]

    def shards(tokens, w_query, w_key, w_value, grad_out):
        fits = (
            w_query.shape[1] == n_seq * HEAD
            and n_seq & (n_seq - 1) == 0
            and n_tp == 4
            and tokens.shape[0] % (CHUNKS * SPAN) == 0
            and tokens.shape[1] % PIECE == 0
        )
        chosen = swapped_shards if fits else ring_shards
        return chosen(tokens, w_query, w_key, w_value, grad_out)

    return jax.shard_map(
        shards, mesh=mesh, in_specs=placed, out_specs=P("seq", None), check_vma=False
    )
```
